32 devices in a mesh: probe: 4 (over y, x), space: 8 (over z, core).
Axes of the slice: x: 2, y: 2, z: 4, core: 2. Of those that a mesh axis runs over, the one named last changes fastest.
Arguments:
- probes: float32 [128, 32768], P('probe', 'space'), may hold values from -6 to 6
- sensitivity: float32 [8, 8, 16384], P(None, None, 'space'), may hold values from -2.1 to 2.1
- obs_weight: float32 [8, 16384], P(None, 'space'), may hold values from 0.5 to 4
- prior_weight: float32 [32768], P('space'), may hold values from 0.2 to 2
- connectivity: int32 [8, 16384], P(None, 'space'), may hold values from 0 to 4351, as said below
Outputs:
- basis: float32 [128, 32768], P('probe', 'space')
- factor: float32 [128, 128], replicated
The draws below stay inside these ranges and needn't reach their ends.
Inputs may be any that keep to these rules, and one draw needn't show every extreme that they name: Each column holds 8 distinct numbers. For an element of the block of device d of space (columns d * 2048 to (d + 1) * 2048 - 1), connectivity + d * 4096 - 128 is an existing node, and the values 0 and 4351 are both named wherever those nodes exist.
All inputs are finite; a program needn't handle non-finite values.
Results may differ from the reference program's by a relative error of at most 0.0003.
Values sent between devices are 32-bit elements; how exact they have to be, the bound alone decides.
A program may use at most 64 MiB of HBM per device.

```python
import math
import jax
import jax.numpy as jnp
from jax import lax

K = 128
ND = 4096
ED = 2048
HALO = 128
GAUSS = 8
NPE = 8
NODES = 32768
ELEMS = 16384


def draw_probes(key, part):
    group_count = K // 16
    key_shared = jax.random.fold_in(key, 11)
    key_scales = jax.random.fold_in(key, 12)
    key_jitter = jax.random.fold_in(key, 13)
    shared = jnp.clip(jax.random.normal(key_shared, (group_count, NODES), jnp.float32), -4.0, 4.0)
    scales = jax.random.uniform(key_scales, (K,), jnp.float32, 0.6, 1.4)
    perturb = jnp.clip(jax.random.normal(key_jitter, (K, NODES), jnp.float32), -4.0, 4.0)
    row_group = jnp.arange(K, dtype=jnp.int32) % group_count
    picked = shared[row_group]
    return (scales[:, None] * picked + 0.01 * perturb).astype(jnp.float32)


def draw_connectivity(key, part):
    element = jnp.arange(ELEMS, dtype=jnp.int32)
    device = element // ED
    local = element - device * ED
    stride = ND // ED
    base_low = device * ND + local * stride
    base_high = base_low + stride
    width = HALO // 4
    slot = jnp.arange(NPE, dtype=jnp.int32)[:, None]
    jitter = jax.random.randint(key, (NPE, ELEMS), 0, width, dtype=jnp.int32)
    jitter = jnp.where((slot == 0) & (local[None, :] == 0), 0, jitter)
    jitter = jnp.where((slot == NPE - 1) & (local[None, :] == ED - 1), width - 1, jitter)
    low_node = base_low[None, :] + slot * width + jitter - HALO
    high_node = base_high[None, :] + (slot - 4) * width + jitter
    node = jnp.where(slot < 4, low_node, high_node)
    node = jnp.where(node < 0, node + 4 * HALO, node)
    node = jnp.where(node >= NODES, node - 4 * HALO, node)
    offsets = device * ND - HALO
    return (node - offsets[None, :]).astype(jnp.int32)


def shard_levels(stream_key, dims, pieces, low, high):
    level, own = 1.0, jax.random.fold_in(stream_key, 6)
    for position, blocks in pieces:
        draws = jnp.exp(jax.random.uniform(jax.random.fold_in(own, position), (blocks,), jnp.float32, low / len(pieces), high / len(pieces)))
        level = level * jnp.repeat(draws, dims[position] // blocks).reshape([-1 if axis == position else 1 for axis in range(len(dims))])
    return level


def scatter_about(rng, dims, deviation, bound, pieces=(), kind=jnp.bfloat16):
    entries = deviation * jax.random.normal(rng, dims, jnp.float32)
    if pieces:
        entries = entries * shard_levels(rng, dims, pieces, -0.22, 0.18)
    return jnp.clip(entries, -bound, bound).astype(kind)


def setup_inputs(seed: int = 0) -> dict:
    seeds = jax.random.split(jax.random.key(seed), 6)
    probes = draw_probes(jax.random.fold_in(seeds[5], 71), 0)
    sensitivity = scatter_about(seeds[1], (GAUSS, NPE, ELEMS), 0.35, 2.1, ((2, 8),), jnp.float32)
    obs_weight = jnp.clip(jnp.exp(math.log(4.0) - 2.0794415 * jax.random.uniform(seeds[2], (GAUSS, ELEMS), jnp.float32) ** shard_levels(seeds[2], (GAUSS, ELEMS), ((1, 8),), -0.2, 0.2)), 0.5, 4.0)
    prior_weight = jnp.clip(jnp.exp(math.log(2.0) - 2.3025851 * jax.random.uniform(seeds[3], (NODES,), jnp.float32) ** shard_levels(seeds[3], (NODES,), ((0, 8),), -0.2, 0.2)), 0.2, 2.0)
    connectivity = draw_connectivity(jax.random.fold_in(seeds[5], 71), 0)
    return {"probes": probes, "sensitivity": sensitivity, "obs_weight": obs_weight, "prior_weight": prior_weight, "connectivity": connectivity}


highest = lax.Precision.HIGHEST

def reference(probes, sensitivity, obs_weight, prior_weight, connectivity):
    element = jnp.arange(ELEMS, dtype=jnp.int32)
    offsets = (element // ED * ND - HALO).astype(jnp.int32)
    node = (connectivity + offsets[None, :]).astype(jnp.int32)

    def apply_column(column):
        gathered = column[node]
        observed = jnp.einsum('gce,ce->ge', sensitivity, gathered, precision=highest) * obs_weight
        pulled = jnp.einsum('gce,ge->ce', sensitivity, observed, precision=highest)
        summed = jnp.zeros((NODES,), jnp.float32).at[node].add(pulled)
        return summed + prior_weight * column
    images = lax.map(apply_column, probes)
    gram_first = jnp.dot(images.astype(jnp.float32), images.T.astype(jnp.float32), precision=highest, preferred_element_type=jnp.float32)
    lower_first = jnp.linalg.cholesky(gram_first)
    basis_first = lax.linalg.triangular_solve(lower_first, images, left_side=True, lower=True)
    gram_second = jnp.dot(basis_first.astype(jnp.float32), basis_first.T.astype(jnp.float32), precision=highest, preferred_element_type=jnp.float32)
    lower_second = jnp.linalg.cholesky(gram_second)
    basis = lax.linalg.triangular_solve(lower_second, basis_first, left_side=True, lower=True)
    scale = jnp.sqrt(jnp.float32(NODES))
    factor = jnp.dot(lower_first.astype(jnp.float32), lower_second.astype(jnp.float32), precision=highest, preferred_element_type=jnp.float32).T
    return (basis * scale, factor / scale)
```

```python
import math

import jax
import jax.numpy as jnp
from jax import lax
from jax.experimental import pallas as pl
from jax.experimental.pallas import tpu as pltpu
from jax.sharding import PartitionSpec as P

HALO = 128


highest = lax.Precision.HIGHEST


def extended_2(block, sides, width):
    for axis, dim in sides:
        count = lax.axis_size(axis)
        forward = [(i, i + 1) for i in range(count - 1)]
        backward = [(target, source) for source, target in forward]
        low = lax.ppermute(
            lax.slice_in_dim(block, block.shape[dim] - width, None, axis=dim), axis, forward
        )
        high = lax.ppermute(lax.slice_in_dim(block, 0, width, axis=dim), axis, backward)
        block = jnp.concatenate([low, block, high], axis=dim)
    return block


def shifted(block, axis, distance):
    devices = range(lax.axis_size(axis))
    route = [(i - distance, i) for i in devices if i - distance in devices]
    return lax.ppermute(block, axis, route)


TILE = 128
WIDE = 256


def split_exact(value):
    high = value.astype(jnp.bfloat16)
    rest = value - high.astype(jnp.float32)
    middle = rest.astype(jnp.bfloat16)
    low = (rest - middle.astype(jnp.float32)).astype(jnp.bfloat16)
    return high, middle, low


def element_kernel(extended, local, sensitivity, weight, out, node, held, pulled, total):
    gauss_count, corner_count, element_count = sensitivity.shape
    rows, nodes = extended.shape
    tiles, wides = nodes // TILE, nodes // WIDE
    total[...] = jnp.zeros_like(total)

    def block(step, carry):
        start = pl.multiple_of(step * WIDE, WIDE)
        for c in range(corner_count):
            index = local[c : c + 1, pl.ds(start, WIDE)]
            node[c] = jnp.broadcast_to(index, (8, WIDE))

        def gather(corner, carry):
            for part in range(WIDE // TILE):
                index = node[corner, :, part * TILE : (part + 1) * TILE]
                lane, tile = index & (TILE - 1), index >> 7
                found = [jnp.zeros((8, TILE), jnp.float32)] * (rows // 8)
                for t in range(tiles):
                    here = tile == t
                    for r in range(rows // 8):
                        source = extended[r * 8 : (r + 1) * 8, t * TILE : (t + 1) * TILE]
                        picked = jnp.take_along_axis(
                            source, lane, axis=1, mode="promise_in_bounds"
                        )
                        found[r] = jnp.where(here, picked, found[r])
                for r in range(rows // 8):
                    held[corner, r * 8 : (r + 1) * 8, part * TILE : (part + 1) * TILE] = found[r]
            return carry

        lax.fori_loop(0, corner_count, gather, 0)

        for part in range(WIDE // TILE):
            lanes = slice(part * TILE, (part + 1) * TILE)
            place = pl.multiple_of(start + part * TILE, TILE)
            for r in range(rows // 16):
                band = slice(r * 16, (r + 1) * 16)
                values = [held[c, band, lanes] for c in range(corner_count)]
                sums = [None] * corner_count
                for g in range(gauss_count):
                    coefficient = [
                        sensitivity[g, c : c + 1, pl.ds(place, TILE)] for c in range(corner_count)
                    ]
                    observed = values[0] * coefficient[0]
                    for c in range(1, corner_count):
                        observed = observed + values[c] * coefficient[c]
                    observed = observed * weight[g : g + 1, pl.ds(place, TILE)]
                    for c in range(corner_count):
                        term = observed * coefficient[c]
                        sums[c] = term if g == 0 else sums[c] + term
                for c in range(corner_count):
                    pulled[c, band, lanes] = sums[c]

        def scatter(corner, carry):
            index = node[corner, 0:1, :]
            lane = jnp.broadcast_to(index & (WIDE - 1), (WIDE, WIDE))
            wide = jnp.broadcast_to(index >> 8, (16, WIDE))
            hot = jnp.where(lax.broadcasted_iota(jnp.int32, (WIDE, WIDE), 0) == lane, 1.0, 0.0)
            hot = hot.astype(jnp.bfloat16)
            hot = jnp.concatenate([hot, hot, hot], axis=1)
            value = jnp.concatenate(split_exact(pulled[corner]), axis=1)
            masked = []
            for h in range(wides):
                mask = jnp.where(wide == h, 1.0, 0.0).astype(jnp.bfloat16)
                mask = jnp.concatenate([mask] * (rows // 16), axis=0)
                masked.append(value * jnp.concatenate([mask] * 3, axis=1))
            masked = jnp.concatenate(masked, axis=0)
            total[...] += lax.dot_general(
                masked, hot, (((1,), (1,)), ((), ())), preferred_element_type=jnp.float32
            )
            return carry

        lax.fori_loop(0, corner_count, scatter, 0)
        return carry

    lax.fori_loop(0, element_count // WIDE, block, 0)
    for h in range(wides):
        out[:, h * WIDE : (h + 1) * WIDE] = total[h * rows : (h + 1) * rows, :]


def padded(array, dim, multiple):
    extra = -array.shape[dim] % multiple
    if not extra:
        return array
    return jnp.pad(array, [(0, extra if d == dim else 0) for d in range(array.ndim)])


def element_images(extended, sensitivity, obs_weight, local):
    probe_count, node_count = extended.shape
    corner_count = local.shape[0]
    extended = padded(padded(extended, 0, 16), 1, WIDE)
    local = padded(local, 1, WIDE)
    sensitivity = padded(sensitivity, 2, WIDE)
    obs_weight = padded(obs_weight, 1, WIDE)
    rows, nodes = extended.shape
    vmem = pl.BlockSpec(memory_space=pltpu.VMEM)
    summed = pl.pallas_call(
        element_kernel,
        out_shape=jax.ShapeDtypeStruct((rows, nodes), jnp.float32),
        in_specs=[vmem] * 4,
        out_specs=vmem,
        scratch_shapes=[
            pltpu.VMEM((corner_count, 8, WIDE), jnp.int32),
            pltpu.VMEM((corner_count, rows, WIDE), jnp.float32),
            pltpu.VMEM((corner_count, rows, WIDE), jnp.float32),
            pltpu.VMEM((nodes // WIDE * rows, WIDE), jnp.float32),
        ],
        compiler_params=pltpu.CompilerParams(vmem_limit_bytes=48 * 1024 * 1024),
        name="elements",
    )(extended, local, sensitivity, obs_weight)
    return summed[:probe_count, :node_count]


def gram_over_space(partial_value):
    return lax.psum(partial_value, "space")


def orthonormal(rows, reduce_gram):
    gram_first = reduce_gram(
        jnp.dot(rows, rows.T, precision=highest, preferred_element_type=jnp.float32)
    )
    lower_first = jnp.linalg.cholesky(gram_first)
    basis_first = lax.linalg.triangular_solve(lower_first, rows, left_side=True, lower=True)
    gram_second = reduce_gram(
        jnp.dot(basis_first, basis_first.T, precision=highest, preferred_element_type=jnp.float32)
    )
    lower_second = jnp.linalg.cholesky(gram_second)
    basis = lax.linalg.triangular_solve(lower_second, basis_first, left_side=True, lower=True)
    factor = jnp.dot(
        lower_first, lower_second, precision=highest, preferred_element_type=jnp.float32
    ).T
    return (basis, factor)


def on_device(probes, sensitivity, obs_weight, prior_weight, connectivity):
    node_count = probes.shape[1]
    probe_count = probes.shape[0]
    extended = extended_2(probes, (("space", 1),), HALO)
    summed = element_images(extended, sensitivity, obs_weight, connectivity)
    lower_rim = shifted(summed[:, :HALO], "space", -1)
    upper_rim = shifted(summed[:, HALO + node_count :], "space", 1)
    images = summed[:, HALO : HALO + node_count] + prior_weight[None, :] * probes
    images = images.at[:, node_count - HALO :].add(lower_rim)
    images = images.at[:, :HALO].add(upper_rim)
    scale = math.sqrt(float(node_count * lax.axis_size("space")))
    whole = lax.all_gather(images, "probe", axis=0, tiled=True)
    basis, factor = orthonormal(whole, gram_over_space)
    basis = lax.dynamic_slice_in_dim(basis, lax.axis_index("probe") * probe_count, probe_count, 0)
    return (basis * scale, factor / scale)


def solution(mesh):
    return jax.shard_map(
        on_device,
        mesh=mesh,
        in_specs=(
            P("probe", "space"),
            P(None, None, "space"),
            P(None, "space"),
            P("space"),
            P(None, "space"),
        ),
        out_specs=(P("probe", "space"), P()),
        check_vma=False,
    )
```

```python
import functools
import math

import jax
import jax.numpy as jnp
from jax import lax
from jax.experimental import pallas as pl
from jax.experimental.pallas import tpu as pltpu
from jax.sharding import PartitionSpec as P

HALO = 128


highest = lax.Precision.HIGHEST


def extended_2(block, sides, width):
    for axis, dim in sides:
        count = lax.axis_size(axis)
        forward = [(i, i + 1) for i in range(count - 1)]
        backward = [(target, source) for source, target in forward]
        low = lax.ppermute(
            lax.slice_in_dim(block, block.shape[dim] - width, None, axis=dim), axis, forward
        )
        high = lax.ppermute(lax.slice_in_dim(block, 0, width, axis=dim), axis, backward)
        block = jnp.concatenate([low, block, high], axis=dim)
    return block


TILE = 128
WIDE = 256


def split_exact(value):
    high = value.astype(jnp.bfloat16)
    rest = value - high.astype(jnp.float32)
    middle = rest.astype(jnp.bfloat16)
    low = (rest - middle.astype(jnp.float32)).astype(jnp.bfloat16)
    return high, middle, low


def element_kernel(extended, local, sensitivity, weight, out, node, held, pulled, total):
    gauss_count, corner_count, element_count = sensitivity.shape
    rows, nodes = extended.shape
    tiles, wides = nodes // TILE, nodes // WIDE
    total[...] = jnp.zeros_like(total)

    def block(step, carry):
        start = pl.multiple_of(step * WIDE, WIDE)
        for c in range(corner_count):
            index = local[c : c + 1, pl.ds(start, WIDE)]
            node[c] = jnp.broadcast_to(index, (8, WIDE))

        def gather(corner, carry):
            for part in range(WIDE // TILE):
                index = node[corner, :, part * TILE : (part + 1) * TILE]
                lane, tile = index & (TILE - 1), index >> 7
                found = [jnp.zeros((8, TILE), jnp.float32)] * (rows // 8)
                for t in range(tiles):
                    here = tile == t
                    for r in range(rows // 8):
                        source = extended[r * 8 : (r + 1) * 8, t * TILE : (t + 1) * TILE]
                        picked = jnp.take_along_axis(
                            source, lane, axis=1, mode="promise_in_bounds"
                        )
                        found[r] = jnp.where(here, picked, found[r])
                for r in range(rows // 8):
                    held[corner, r * 8 : (r + 1) * 8, part * TILE : (part + 1) * TILE] = found[r]
            return carry

        lax.fori_loop(0, corner_count, gather, 0)

        for part in range(WIDE // TILE):
            lanes = slice(part * TILE, (part + 1) * TILE)
            place = pl.multiple_of(start + part * TILE, TILE)
            for r in range(rows // 16):
                band = slice(r * 16, (r + 1) * 16)
                values = [held[c, band, lanes] for c in range(corner_count)]
                sums = [None] * corner_count
                for g in range(gauss_count):
                    coefficient = [
                        sensitivity[g, c : c + 1, pl.ds(place, TILE)] for c in range(corner_count)
                    ]
                    observed = values[0] * coefficient[0]
                    for c in range(1, corner_count):
                        observed = observed + values[c] * coefficient[c]
                    observed = observed * weight[g : g + 1, pl.ds(place, TILE)]
                    for c in range(corner_count):
                        term = observed * coefficient[c]
                        sums[c] = term if g == 0 else sums[c] + term
                for c in range(corner_count):
                    pulled[c, band, lanes] = sums[c]

        def scatter(corner, carry):
            index = node[corner, 0:1, :]
            lane = jnp.broadcast_to(index & (WIDE - 1), (WIDE, WIDE))
            wide = jnp.broadcast_to(index >> 8, (16, WIDE))
            hot = jnp.where(lax.broadcasted_iota(jnp.int32, (WIDE, WIDE), 0) == lane, 1.0, 0.0)
            hot = hot.astype(jnp.bfloat16)
            hot = jnp.concatenate([hot, hot, hot], axis=1)
            value = jnp.concatenate(split_exact(pulled[corner]), axis=1)
            masked = []
            for h in range(wides):
                mask = jnp.where(wide == h, 1.0, 0.0).astype(jnp.bfloat16)
                mask = jnp.concatenate([mask] * (rows // 16), axis=0)
                masked.append(value * jnp.concatenate([mask] * 3, axis=1))
            masked = jnp.concatenate(masked, axis=0)
            total[...] += lax.dot_general(
                masked, hot, (((1,), (1,)), ((), ())), preferred_element_type=jnp.float32
            )
            return carry

        lax.fori_loop(0, corner_count, scatter, 0)
        return carry

    lax.fori_loop(0, element_count // WIDE, block, 0)
    for h in range(wides):
        out[:, h * WIDE : (h + 1) * WIDE] = total[h * rows : (h + 1) * rows, :]


def padded(array, dim, multiple):
    extra = -array.shape[dim] % multiple
    if not extra:
        return array
    return jnp.pad(array, [(0, extra if d == dim else 0) for d in range(array.ndim)])


def element_images(extended, sensitivity, obs_weight, local):
    probe_count, node_count = extended.shape
    corner_count = local.shape[0]
    extended = padded(padded(extended, 0, 16), 1, WIDE)
    local = padded(local, 1, WIDE)
    sensitivity = padded(sensitivity, 2, WIDE)
    obs_weight = padded(obs_weight, 1, WIDE)
    rows, nodes = extended.shape
    vmem = pl.BlockSpec(memory_space=pltpu.VMEM)
    summed = pl.pallas_call(
        element_kernel,
        out_shape=jax.ShapeDtypeStruct((rows, nodes), jnp.float32),
        in_specs=[vmem] * 4,
        out_specs=vmem,
        scratch_shapes=[
            pltpu.VMEM((corner_count, 8, WIDE), jnp.int32),
            pltpu.VMEM((corner_count, rows, WIDE), jnp.float32),
            pltpu.VMEM((corner_count, rows, WIDE), jnp.float32),
            pltpu.VMEM((nodes // WIDE * rows, WIDE), jnp.float32),
        ],
        compiler_params=pltpu.CompilerParams(vmem_limit_bytes=48 * 1024 * 1024),
        name="elements",
    )(extended, local, sensitivity, obs_weight)
    return summed[:probe_count, :node_count]


MESH = pl.DeviceIdType.MESH
BAND = 8


def exact_dot(left, right, left_dim=1, right_dim=0):
    return lax.dot_general(
        left,
        right,
        (((left_dim,), (right_dim,)), ((), ())),
        precision=highest,
        preferred_element_type=jnp.float32,
    )


def small_factor(columns):
    entry = {}
    for m in range(BAND):
        for i in range(m, BAND):
            entry[i, m] = jnp.broadcast_to(columns[m][i : i + 1, :], columns[m].shape)
    inverse = {}
    for m in range(BAND):
        root = lax.rsqrt(entry[m, m])
        for i in range(m + 1, BAND):
            entry[i, m] = entry[i, m] * root
        for i in range(m + 1, BAND):
            for k in range(m + 1, i + 1):
                entry[i, k] = entry[i, k] - entry[i, m] * entry[k, m]
        for k in range(m):
            term = entry[m, k] * inverse[k, k]
            for n in range(k + 1, m):
                term = term + entry[m, n] * inverse[n, k]
            inverse[m, k] = -term * root
        inverse[m, m] = root
    return inverse


def factored(gram):
    size = gram.shape[0]
    row = lax.broadcasted_iota(jnp.int32, (size, size), 0)
    column = lax.broadcasted_iota(jnp.int32, (size, size), 1)
    unit = jnp.where(row == column, 1.0, 0.0)
    level = lax.broadcasted_iota(jnp.int32, (BAND, size), 0)
    bands = []
    for j in range(size // BAND):
        part = slice(j * BAND, (j + 1) * BAND)
        bands.append((gram[part], unit[part]))
    for j in range(size // BAND):
        left, right = bands[j]
        columns = [
            jnp.broadcast_to(left[:, j * BAND + m : j * BAND + m + 1], left.shape)
            for m in range(BAND)
        ]
        inverse = small_factor(columns)
        new_left = new_right = None
        for m in range(BAND):
            weights = jnp.zeros_like(left)
            for i in range(m, BAND):
                weights = jnp.where(level == i, inverse[i, m], weights)
            add_left = weights * left[m : m + 1, :]
            add_right = weights * right[m : m + 1, :]
            new_left = add_left if m == 0 else new_left + add_left
            new_right = add_right if m == 0 else new_right + add_right
        bands[j] = (new_left, new_right)
        if (j + 1) * BAND < size:
            multipliers = new_left.T
            away_left = exact_dot(multipliers, new_left)
            away_right = exact_dot(multipliers, new_right)
            for i in range(j + 1, size // BAND):
                part = slice(i * BAND, (i + 1) * BAND)
                bands[i] = (bands[i][0] - away_left[part], bands[i][1] - away_right[part])
    upper = jnp.concatenate([band[0] for band in bands], axis=0)
    lower = jnp.concatenate([band[1] for band in bands], axis=0)
    return jnp.where(row <= column, upper, 0.0), lower


def send_all(axis, count, me, source, target, send_sem, recv_sem):
    copies = []
    for d in range(1, count):
        to = lax.rem(me + d, count)
        copy = pltpu.make_async_remote_copy(
            src_ref=source(to),
            dst_ref=target,
            send_sem=send_sem.at[d],
            recv_sem=recv_sem.at[d],
            device_id={axis: to},
            device_id_type=MESH,
        )
        copy.start()
        copies.append(copy)
    return copies


def wait_all(copies):
    for copy in copies:
        copy.wait()


def orthonormal_kernel(
    probe_axis_size, space_axis_size, summed, probes, prior, basis, factor,
    images, rim, mine, block, ready, partial, strips, bands, grams,
    rim_send, rim_recv, move_send, move_recv, a_send, a_recv, b_send, b_recv, c_send, c_recv,
):
    p_me, s_me = lax.axis_index("probe"), lax.axis_index("space")
    rows, nodes = probes.shape
    size = rows * probe_axis_size
    share = nodes // probe_axis_size
    strip = size // space_axis_size
    halo = (summed.shape[1] - nodes) // 2
    scale = math.sqrt(float(nodes * space_axis_size))

    barrier = pltpu.get_barrier_semaphore()
    for d in range(1, space_axis_size):
        to = lax.rem(s_me + d, space_axis_size)
        pl.semaphore_signal(barrier, inc=1, device_id={"space": to}, device_id_type=MESH)
    for d in range(1, probe_axis_size):
        to = lax.rem(p_me + d, probe_axis_size)
        pl.semaphore_signal(barrier, inc=1, device_id={"probe": to}, device_id_type=MESH)
    pl.semaphore_wait(barrier, space_axis_size + probe_axis_size - 2)

    def rim_copy(side):
        source = summed.at[:, :halo] if side == 0 else summed.at[:, halo + nodes :]
        return pltpu.make_async_remote_copy(
            src_ref=source,
            dst_ref=rim.at[side],
            send_sem=rim_send.at[side],
            recv_sem=rim_recv.at[side],
            device_id={"space": s_me - 1 if side == 0 else s_me + 1},
            device_id_type=MESH,
        )

    has_lower, has_upper = s_me > 0, s_me < space_axis_size - 1
    pl.when(has_lower)(lambda: rim_copy(0).start())
    pl.when(has_upper)(lambda: rim_copy(1).start())
    images[...] = summed[:, halo : halo + nodes] + prior[...] * probes[...]

    @pl.when(has_upper)
    def _():
        rim_copy(0).wait_recv()
        images[:, nodes - halo :] += rim[0]

    @pl.when(has_lower)
    def _():
        rim_copy(1).wait_recv()
        images[:, :halo] += rim[1]

    def lanes(index):
        return pl.ds(pl.multiple_of(index * share, share), share)

    copies = send_all(
        "probe", probe_axis_size, p_me, lambda to: images.at[:, lanes(to)],
        mine.at[p_me], move_send.at[0], move_recv.at[0],
    )
    mine[p_me] = images[:, lanes(p_me)]
    wait_all(copies)

    def summed_gram(turn, value):
        for s in range(space_axis_size):
            partial[turn, s] = value[s * strip : (s + 1) * strip]
        copies = send_all(
            "space", space_axis_size, s_me, lambda to: partial.at[turn, to],
            strips.at[turn, s_me], a_send.at[turn], a_recv.at[turn],
        )
        strips[turn, s_me] = partial[turn, s_me]
        wait_all(copies)
        total = strips[turn, 0]
        for s in range(1, space_axis_size):
            total = total + strips[turn, s]
        bands[turn, p_me] = total
        copies = send_all(
            "probe", probe_axis_size, p_me, lambda to: bands.at[turn, p_me],
            bands.at[turn, p_me], b_send.at[turn], b_recv.at[turn],
        )
        wait_all(copies)
        total = bands[turn, 0]
        for p in range(1, probe_axis_size):
            total = total + bands[turn, p]
        grams[turn, s_me] = total
        copies = send_all(
            "space", space_axis_size, s_me, lambda to: grams.at[turn, s_me],
            grams.at[turn, s_me], c_send.at[turn], c_recv.at[turn],
        )
        wait_all(copies)
        return jnp.concatenate([grams[turn, s] for s in range(space_axis_size)], axis=0)

    whole = mine[...].reshape(size, share)
    upper_first, inverse_first = factored(summed_gram(0, exact_dot(whole, whole, 1, 1)))
    block[...] = exact_dot(inverse_first, mine[...].reshape(size, share))
    first = block[...]
    upper_second, inverse_second = factored(summed_gram(1, exact_dot(first, first, 1, 1)))
    done = exact_dot(inverse_second * scale, block[...])
    ready[...] = done.reshape(probe_axis_size, rows, share)
    copies = send_all(
        "probe", probe_axis_size, p_me, lambda to: ready.at[to],
        basis.at[:, lanes(p_me)], move_send.at[1], move_recv.at[1],
    )
    basis[:, lanes(p_me)] = ready[p_me]
    factor[...] = exact_dot(upper_second, upper_first) / scale
    wait_all(copies)
    pl.when(has_lower)(lambda: rim_copy(0).wait_send())
    pl.when(has_upper)(lambda: rim_copy(1).wait_send())


def orthonormal(summed, probes, prior):
    probe_axis_size, space_axis_size = lax.axis_size("probe"), lax.axis_size("space")
    rows, nodes = probes.shape
    halo = (summed.shape[1] - nodes) // 2
    size, share = rows * probe_axis_size, nodes // probe_axis_size
    strip = size // space_axis_size
    vmem = pl.BlockSpec(memory_space=pltpu.VMEM)
    dma = pltpu.SemaphoreType.DMA
    return pl.pallas_call(
        functools.partial(orthonormal_kernel, probe_axis_size, space_axis_size),
        out_shape=(
            jax.ShapeDtypeStruct((rows, nodes), jnp.float32),
            jax.ShapeDtypeStruct((size, size), jnp.float32),
        ),
        in_specs=[vmem] * 3,
        out_specs=(vmem, vmem),
        scratch_shapes=[
            pltpu.VMEM((rows, nodes), jnp.float32),
            pltpu.VMEM((2, rows, halo), jnp.float32),
            pltpu.VMEM((probe_axis_size, rows, share), jnp.float32),
            pltpu.VMEM((size, share), jnp.float32),
            pltpu.VMEM((probe_axis_size, rows, share), jnp.float32),
            pltpu.VMEM((2, space_axis_size, strip, size), jnp.float32),
            pltpu.VMEM((2, space_axis_size, strip, size), jnp.float32),
            pltpu.VMEM((2, probe_axis_size, strip, size), jnp.float32),
            pltpu.VMEM((2, space_axis_size, strip, size), jnp.float32),
            dma((2,)),
            dma((2,)),
            dma((2, probe_axis_size)),
            dma((2, probe_axis_size)),
            dma((2, space_axis_size)),
            dma((2, space_axis_size)),
            dma((2, probe_axis_size)),
            dma((2, probe_axis_size)),
            dma((2, space_axis_size)),
            dma((2, space_axis_size)),
        ],
        compiler_params=pltpu.CompilerParams(
            collective_id=0, has_side_effects=True, vmem_limit_bytes=48 * 1024 * 1024
        ),
        name="orthonormal",
    )(summed, probes, prior)


def on_device(probes, sensitivity, obs_weight, prior_weight, connectivity):
    extended = extended_2(probes, (("space", 1),), HALO)
    summed = element_images(extended, sensitivity, obs_weight, connectivity)
    return orthonormal(summed, probes, prior_weight[None, :])


def solution(mesh):
    return jax.shard_map(
        on_device,
        mesh=mesh,
        in_specs=(
            P("probe", "space"),
            P(None, None, "space"),
            P(None, "space"),
            P("space"),
            P(None, "space"),
        ),
        out_specs=(P("probe", "space"), P()),
        check_vma=False,
    )
```

```python
import functools
import math

import jax
import jax.numpy as jnp
from jax import lax
from jax.experimental import pallas as pl
from jax.experimental.pallas import tpu as pltpu
from jax.sharding import PartitionSpec as P

HALO = 128


highest = lax.Precision.HIGHEST


TILE = 128
WIDE = 256


def split_exact(value):
    high = value.astype(jnp.bfloat16)
    rest = value - high.astype(jnp.float32)
    middle = rest.astype(jnp.bfloat16)
    low = (rest - middle.astype(jnp.float32)).astype(jnp.bfloat16)
    return high, middle, low


MESH = pl.DeviceIdType.MESH


def element_kernel(
    extended, local, corner_column, sensitivity, weight, out, node, spread, held, pulled, total
):
    gauss_count, corner_count, element_count = sensitivity.shape
    rows, nodes = extended.shape
    tiles, wides = nodes // TILE, nodes // WIDE
    blocks = element_count // WIDE
    total[...] = jnp.zeros_like(total)

    def load_nodes(step, turn):
        start = pl.multiple_of(step * WIDE, WIDE)
        for c in range(corner_count):
            index = local[c : c + 1, pl.ds(start, WIDE)]
            node[turn, c] = jnp.broadcast_to(index, (16, WIDE))

    def load_columns(step):
        start = pl.multiple_of(step * WIDE, WIDE)
        for c in range(corner_count):
            column = corner_column[pl.ds(start, WIDE), c : c + 1]
            spread[c] = jnp.broadcast_to(column & (WIDE - 1), (WIDE, TILE))

    def gather(corner, turn):
        for part in range(WIDE // TILE):
            lanes = slice(part * TILE, (part + 1) * TILE)
            index = node[turn, corner, 0:8, lanes]
            lane, tile = index & (TILE - 1), index >> 7
            found = [jnp.zeros((8, TILE), jnp.float32)] * (rows // 8)
            for t in range(tiles):
                here = tile == t
                for r in range(rows // 8):
                    source = extended[r * 8 : (r + 1) * 8, t * TILE : (t + 1) * TILE]
                    picked = jnp.take_along_axis(source, lane, axis=1, mode="promise_in_bounds")
                    found[r] = jnp.where(here, picked, found[r])
            for r in range(rows // 8):
                held[corner, r * 8 : (r + 1) * 8, lanes] = found[r]

    def scatter(corner, turn):
        wide = node[turn, corner] >> 8
        lane = spread[corner]
        count = lax.broadcasted_iota(jnp.int32, (WIDE, TILE), 1)
        hot = jnp.concatenate(
            [
                jnp.where(lane == count + part * TILE, 1.0, 0.0).astype(jnp.bfloat16)
                for part in range(WIDE // TILE)
            ],
            axis=1,
        )
        hot = jnp.concatenate([hot, hot, hot], axis=0)
        value = jnp.concatenate(split_exact(pulled[corner]), axis=1)
        masked = []
        for h in range(wides):
            mask = jnp.where(wide == h, 1.0, 0.0).astype(jnp.bfloat16)
            mask = jnp.concatenate([mask] * (rows // 16), axis=0)
            masked.append(value * jnp.concatenate([mask] * 3, axis=1))
        masked = jnp.concatenate(masked, axis=0)
        total[...] += jnp.dot(masked, hot, preferred_element_type=jnp.float32)

    def elements(step):
        for part in range(WIDE // TILE):
            lanes = slice(part * TILE, (part + 1) * TILE)
            place = pl.multiple_of(step * WIDE + part * TILE, TILE)
            for r in range(rows // 16):
                band = slice(r * 16, (r + 1) * 16)
                values = [held[c, band, lanes] for c in range(corner_count)]
                sums = [None] * corner_count
                for g in range(gauss_count):
                    coefficient = [
                        sensitivity[g, c : c + 1, pl.ds(place, TILE)] for c in range(corner_count)
                    ]
                    observed = values[0] * coefficient[0]
                    for c in range(1, corner_count):
                        observed = observed + values[c] * coefficient[c]
                    observed = observed * weight[g : g + 1, pl.ds(place, TILE)]
                    for c in range(corner_count):
                        term = observed * coefficient[c]
                        sums[c] = term if g == 0 else sums[c] + term
                for c in range(corner_count):
                    pulled[c, band, lanes] = sums[c]

    load_nodes(0, 0)

    def first(corner, carry):
        gather(corner, 0)
        return carry

    lax.fori_loop(0, corner_count, first, 0)

    def block(step, carry):
        turn = lax.rem(step, 2)
        elements(step)
        load_columns(step)
        load_nodes(jnp.minimum(step + 1, blocks - 1), 1 - turn)

        def both(corner, carry):
            scatter(corner, turn)
            gather(corner, 1 - turn)
            return carry

        lax.fori_loop(0, corner_count, both, 0)
        return carry

    lax.fori_loop(0, blocks, block, 0)
    for h in range(wides):
        out[:, h * WIDE : (h + 1) * WIDE] = total[h * rows : (h + 1) * rows, :]


def padded(array, dim, multiple):
    extra = -array.shape[dim] % multiple
    if not extra:
        return array
    return jnp.pad(array, [(0, extra if d == dim else 0) for d in range(array.ndim)])


def element_images(extended, sensitivity, obs_weight, local):
    corner_count = local.shape[0]
    local = padded(local, 1, WIDE)
    sensitivity = padded(sensitivity, 2, WIDE)
    obs_weight = padded(obs_weight, 1, WIDE)
    rows, nodes = extended.shape
    vmem = pl.BlockSpec(memory_space=pltpu.VMEM)
    return pl.pallas_call(
        element_kernel,
        out_shape=jax.ShapeDtypeStruct((rows, nodes), jnp.float32),
        in_specs=[vmem] * 5,
        out_specs=vmem,
        scratch_shapes=[
            pltpu.VMEM((2, corner_count, 16, WIDE), jnp.int32),
            pltpu.VMEM((corner_count, WIDE, TILE), jnp.int32),
            pltpu.VMEM((corner_count, rows, WIDE), jnp.float32),
            pltpu.VMEM((corner_count, rows, WIDE), jnp.float32),
            pltpu.VMEM((nodes // WIDE * rows, WIDE), jnp.float32),
        ],
        compiler_params=pltpu.CompilerParams(vmem_limit_bytes=48 * 1024 * 1024),
        name="elements",
    )(extended, local, local.T, sensitivity, obs_weight)


def halo_kernel(space_axis_size, halo, probes, extended, send_sem, recv_sem):
    s_me = lax.axis_index("space")
    rows, nodes = probes.shape
    has_lower, has_upper = s_me > 0, s_me < space_axis_size - 1
    barrier = pltpu.get_barrier_semaphore()

    def greet(to):
        pl.semaphore_signal(barrier, inc=1, device_id={"space": to}, device_id_type=MESH)

    pl.when(has_lower)(lambda: greet(s_me - 1))
    pl.when(has_upper)(lambda: greet(s_me + 1))
    pl.semaphore_wait(barrier, jnp.where(has_lower, 1, 0) + jnp.where(has_upper, 1, 0))

    def copy(side):
        low = side == 0
        return pltpu.make_async_remote_copy(
            src_ref=probes.at[:, :halo] if low else probes.at[:, nodes - halo :],
            dst_ref=extended.at[:rows, halo + nodes : halo + nodes + halo]
            if low
            else extended.at[:rows, :halo],
            send_sem=send_sem.at[side],
            recv_sem=recv_sem.at[side],
            device_id={"space": s_me - 1 if low else s_me + 1},
            device_id_type=MESH,
        )

    pl.when(has_lower)(lambda: copy(0).start())
    pl.when(has_upper)(lambda: copy(1).start())
    extended[:rows, halo : halo + nodes] = probes[...]
    if extended.shape[0] > rows:
        extended[rows:, :] = jnp.zeros_like(extended[rows:, :])
    end = halo + nodes + halo
    if extended.shape[1] > end:
        extended[:rows, end:] = jnp.zeros_like(extended[:rows, end:])

    @pl.when(jnp.logical_not(has_lower))
    def _():
        extended[:rows, :halo] = jnp.zeros((rows, halo), jnp.float32)

    @pl.when(jnp.logical_not(has_upper))
    def _():
        extended[:rows, halo + nodes : end] = jnp.zeros((rows, halo), jnp.float32)

    @pl.when(has_lower)
    def _():
        copy(1).wait_recv()
        copy(0).wait_send()

    @pl.when(has_upper)
    def _():
        copy(0).wait_recv()
        copy(1).wait_send()


def with_halo(probes, halo):
    space_axis_size = lax.axis_size("space")
    rows, nodes = probes.shape
    vmem = pl.BlockSpec(memory_space=pltpu.VMEM)
    return pl.pallas_call(
        functools.partial(halo_kernel, space_axis_size, halo),
        out_shape=jax.ShapeDtypeStruct(
            (rows + -rows % 16, nodes + 2 * halo + -(nodes + 2 * halo) % WIDE), jnp.float32
        ),
        in_specs=[vmem],
        out_specs=vmem,
        scratch_shapes=[pltpu.SemaphoreType.DMA((2,)), pltpu.SemaphoreType.DMA((2,))],
        compiler_params=pltpu.CompilerParams(
            collective_id=1, has_side_effects=True, vmem_limit_bytes=16 * 1024 * 1024
        ),
        name="halo",
    )(probes)


BAND = 8


def exact_dot(left, right, left_dim=1, right_dim=0):
    return lax.dot_general(
        left,
        right,
        (((left_dim,), (right_dim,)), ((), ())),
        precision=highest,
        preferred_element_type=jnp.float32,
    )


def small_factor(columns):
    entry = {}
    for m in range(BAND):
        for i in range(m, BAND):
            entry[i, m] = jnp.broadcast_to(columns[m][i : i + 1, :], columns[m].shape)
    inverse = {}
    for m in range(BAND):
        root = lax.rsqrt(entry[m, m])
        for i in range(m + 1, BAND):
            entry[i, m] = entry[i, m] * root
        for i in range(m + 1, BAND):
            for k in range(m + 1, i + 1):
                entry[i, k] = entry[i, k] - entry[i, m] * entry[k, m]
        for k in range(m):
            term = entry[m, k] * inverse[k, k]
            for n in range(k + 1, m):
                term = term + entry[m, n] * inverse[n, k]
            inverse[m, k] = -term * root
        inverse[m, m] = root
    return inverse


def factored(gram):
    size = gram.shape[0]
    row = lax.broadcasted_iota(jnp.int32, (size, size), 0)
    column = lax.broadcasted_iota(jnp.int32, (size, size), 1)
    unit = jnp.where(row == column, 1.0, 0.0)
    level = lax.broadcasted_iota(jnp.int32, (BAND, size), 0)
    bands = []
    for j in range(size // BAND):
        part = slice(j * BAND, (j + 1) * BAND)
        bands.append((gram[part], unit[part]))
    for j in range(size // BAND):
        left, right = bands[j]
        columns = [
            jnp.broadcast_to(left[:, j * BAND + m : j * BAND + m + 1], left.shape)
            for m in range(BAND)
        ]
        inverse = small_factor(columns)
        new_left = new_right = None
        for m in range(BAND):
            weights = jnp.zeros_like(left)
            for i in range(m, BAND):
                weights = jnp.where(level == i, inverse[i, m], weights)
            add_left = weights * left[m : m + 1, :]
            add_right = weights * right[m : m + 1, :]
            new_left = add_left if m == 0 else new_left + add_left
            new_right = add_right if m == 0 else new_right + add_right
        bands[j] = (new_left, new_right)
        if (j + 1) * BAND < size:
            multipliers = new_left.T
            away_left = exact_dot(multipliers, new_left)
            away_right = exact_dot(multipliers, new_right)
            for i in range(j + 1, size // BAND):
                part = slice(i * BAND, (i + 1) * BAND)
                bands[i] = (bands[i][0] - away_left[part], bands[i][1] - away_right[part])
    upper = jnp.concatenate([band[0] for band in bands], axis=0)
    lower = jnp.concatenate([band[1] for band in bands], axis=0)
    return jnp.where(row <= column, upper, 0.0), lower


def send_all(axis, count, me, source, target, send_sem, recv_sem):
    copies = []
    for d in range(1, count):
        to = lax.rem(me + d, count)
        copy = pltpu.make_async_remote_copy(
            src_ref=source(to),
            dst_ref=target,
            send_sem=send_sem.at[d],
            recv_sem=recv_sem.at[d],
            device_id={axis: to},
            device_id_type=MESH,
        )
        copy.start()
        copies.append(copy)
    return copies


def wait_all(copies):
    for copy in copies:
        copy.wait()


def orthonormal_kernel(
    probe_axis_size, space_axis_size, halo, summed, probes, prior, basis, factor,
    images, rim, mine, block, ready, partial, strips, bands, grams,
    rim_send, rim_recv, move_send, move_recv, a_send, a_recv, b_send, b_recv, c_send, c_recv,
):
    p_me, s_me = lax.axis_index("probe"), lax.axis_index("space")
    rows, nodes = probes.shape
    size = rows * probe_axis_size
    share = nodes // probe_axis_size
    strip = size // space_axis_size
    scale = math.sqrt(float(nodes * space_axis_size))

    barrier = pltpu.get_barrier_semaphore()
    for d in range(1, space_axis_size):
        to = lax.rem(s_me + d, space_axis_size)
        pl.semaphore_signal(barrier, inc=1, device_id={"space": to}, device_id_type=MESH)
    for d in range(1, probe_axis_size):
        to = lax.rem(p_me + d, probe_axis_size)
        pl.semaphore_signal(barrier, inc=1, device_id={"probe": to}, device_id_type=MESH)
    pl.semaphore_wait(barrier, space_axis_size + probe_axis_size - 2)

    end = halo + nodes + halo

    def rim_copy(side):
        source = summed.at[:rows, :halo] if side == 0 else summed.at[:rows, halo + nodes : end]
        return pltpu.make_async_remote_copy(
            src_ref=source,
            dst_ref=rim.at[side],
            send_sem=rim_send.at[side],
            recv_sem=rim_recv.at[side],
            device_id={"space": s_me - 1 if side == 0 else s_me + 1},
            device_id_type=MESH,
        )

    has_lower, has_upper = s_me > 0, s_me < space_axis_size - 1
    pl.when(has_lower)(lambda: rim_copy(0).start())
    pl.when(has_upper)(lambda: rim_copy(1).start())
    images[...] = summed[:rows, halo : halo + nodes] + prior[...] * probes[...]

    @pl.when(has_upper)
    def _():
        rim_copy(0).wait_recv()
        images[:, nodes - halo :] += rim[0]

    @pl.when(has_lower)
    def _():
        rim_copy(1).wait_recv()
        images[:, :halo] += rim[1]

    def lanes(index):
        return pl.ds(pl.multiple_of(index * share, share), share)

    copies = send_all(
        "probe", probe_axis_size, p_me, lambda to: images.at[:, lanes(to)],
        mine.at[p_me], move_send.at[0], move_recv.at[0],
    )
    mine[p_me] = images[:, lanes(p_me)]
    wait_all(copies)

    def summed_gram(turn, value):
        for s in range(space_axis_size):
            partial[turn, s] = value[s * strip : (s + 1) * strip]
        copies = send_all(
            "space", space_axis_size, s_me, lambda to: partial.at[turn, to],
            strips.at[turn, s_me], a_send.at[turn], a_recv.at[turn],
        )
        strips[turn, s_me] = partial[turn, s_me]
        wait_all(copies)
        total = strips[turn, 0]
        for s in range(1, space_axis_size):
            total = total + strips[turn, s]
        bands[turn, p_me] = total
        copies = send_all(
            "probe", probe_axis_size, p_me, lambda to: bands.at[turn, p_me],
            bands.at[turn, p_me], b_send.at[turn], b_recv.at[turn],
        )
        wait_all(copies)
        total = bands[turn, 0]
        for p in range(1, probe_axis_size):
            total = total + bands[turn, p]
        grams[turn, s_me] = total
        copies = send_all(
            "space", space_axis_size, s_me, lambda to: grams.at[turn, s_me],
            grams.at[turn, s_me], c_send.at[turn], c_recv.at[turn],
        )
        wait_all(copies)
        return jnp.concatenate([grams[turn, s] for s in range(space_axis_size)], axis=0)

    whole = mine[...].reshape(size, share)
    upper_first, inverse_first = factored(summed_gram(0, exact_dot(whole, whole, 1, 1)))
    block[...] = exact_dot(inverse_first, mine[...].reshape(size, share))
    first = block[...]
    upper_second, inverse_second = factored(summed_gram(1, exact_dot(first, first, 1, 1)))
    done = exact_dot(inverse_second * scale, block[...])
    ready[...] = done.reshape(probe_axis_size, rows, share)
    copies = send_all(
        "probe", probe_axis_size, p_me, lambda to: ready.at[to],
        basis.at[:, lanes(p_me)], move_send.at[1], move_recv.at[1],
    )
    basis[:, lanes(p_me)] = ready[p_me]
    factor[...] = exact_dot(upper_second, upper_first) / scale
    wait_all(copies)
    pl.when(has_lower)(lambda: rim_copy(0).wait_send())
    pl.when(has_upper)(lambda: rim_copy(1).wait_send())


def orthonormal(summed, probes, prior, halo):
    probe_axis_size, space_axis_size = lax.axis_size("probe"), lax.axis_size("space")
    rows, nodes = probes.shape
    size, share = rows * probe_axis_size, nodes // probe_axis_size
    strip = size // space_axis_size
    vmem = pl.BlockSpec(memory_space=pltpu.VMEM)
    dma = pltpu.SemaphoreType.DMA
    return pl.pallas_call(
        functools.partial(orthonormal_kernel, probe_axis_size, space_axis_size, halo),
        out_shape=(
            jax.ShapeDtypeStruct((rows, nodes), jnp.float32),
            jax.ShapeDtypeStruct((size, size), jnp.float32),
        ),
        in_specs=[vmem] * 3,
        out_specs=(vmem, vmem),
        scratch_shapes=[
            pltpu.VMEM((rows, nodes), jnp.float32),
            pltpu.VMEM((2, rows, halo), jnp.float32),
            pltpu.VMEM((probe_axis_size, rows, share), jnp.float32),
            pltpu.VMEM((size, share), jnp.float32),
            pltpu.VMEM((probe_axis_size, rows, share), jnp.float32),
            pltpu.VMEM((2, space_axis_size, strip, size), jnp.float32),
            pltpu.VMEM((2, space_axis_size, strip, size), jnp.float32),
            pltpu.VMEM((2, probe_axis_size, strip, size), jnp.float32),
            pltpu.VMEM((2, space_axis_size, strip, size), jnp.float32),
            dma((2,)),
            dma((2,)),
            dma((2, probe_axis_size)),
            dma((2, probe_axis_size)),
            dma((2, space_axis_size)),
            dma((2, space_axis_size)),
            dma((2, probe_axis_size)),
            dma((2, probe_axis_size)),
            dma((2, space_axis_size)),
            dma((2, space_axis_size)),
        ],
        compiler_params=pltpu.CompilerParams(
            collective_id=0, has_side_effects=True, vmem_limit_bytes=48 * 1024 * 1024
        ),
        name="orthonormal",
    )(summed, probes, prior)


def on_device(probes, sensitivity, obs_weight, prior_weight, connectivity):
    extended = with_halo(probes, HALO)
    summed = element_images(extended, sensitivity, obs_weight, connectivity)
    return orthonormal(summed, probes, prior_weight[None, :], HALO)


def solution(mesh):
    return jax.shard_map(
        on_device,
        mesh=mesh,
        in_specs=(
            P("probe", "space"),
            P(None, None, "space"),
            P(None, "space"),
            P("space"),
            P(None, "space"),
        ),
        out_specs=(P("probe", "space"), P()),
        check_vma=False,
    )
```

```python
import functools
import math

import jax
import jax.numpy as jnp
from jax import lax
from jax.experimental import pallas as pl
from jax.experimental.pallas import tpu as pltpu
from jax.sharding import PartitionSpec as P

HALO = 128


highest = lax.Precision.HIGHEST


TILE = 128
WIDE = 256


def split_exact(value):
    high = value.astype(jnp.bfloat16)
    rest = value - high.astype(jnp.float32)
    middle = rest.astype(jnp.bfloat16)
    low = (rest - middle.astype(jnp.float32)).astype(jnp.bfloat16)
    return high, middle, low


MESH = pl.DeviceIdType.MESH


def element_kernel(
    extended, local, corner_column, sensitivity, weight, out, node, spread, held, pulled, total
):
    gauss_count, corner_count, element_count = sensitivity.shape
    rows, nodes = extended.shape
    tiles, wides = nodes // TILE, nodes // WIDE
    blocks = element_count // WIDE
    total[...] = jnp.zeros_like(total)

    def load_nodes(step, turn):
        start = pl.multiple_of(step * WIDE, WIDE)
        for c in range(corner_count):
            index = local[c : c + 1, pl.ds(start, WIDE)]
            node[turn, c] = jnp.broadcast_to(index, (16, WIDE))

    def load_columns(step):
        start = pl.multiple_of(step * WIDE, WIDE)
        for c in range(corner_count):
            column = corner_column[pl.ds(start, WIDE), c : c + 1]
            spread[c] = jnp.broadcast_to(column & (WIDE - 1), (WIDE, TILE))

    def gather(corner, turn):
        for part in range(WIDE // TILE):
            lanes = slice(part * TILE, (part + 1) * TILE)
            index = node[turn, corner, 0:8, lanes]
            lane, tile = index & (TILE - 1), index >> 7
            found = [jnp.zeros((8, TILE), jnp.float32)] * (rows // 8)
            for t in range(tiles):
                here = tile == t
                for r in range(rows // 8):
                    source = extended[r * 8 : (r + 1) * 8, t * TILE : (t + 1) * TILE]
                    picked = jnp.take_along_axis(source, lane, axis=1, mode="promise_in_bounds")
                    found[r] = jnp.where(here, picked, found[r])
            for r in range(rows // 8):
                held[corner, r * 8 : (r + 1) * 8, lanes] = found[r]

    def scatter(corner, turn):
        wide = node[turn, corner] >> 8
        lane = spread[corner]
        count = lax.broadcasted_iota(jnp.int32, (WIDE, TILE), 1)
        hot = jnp.concatenate(
            [
                jnp.where(lane == count + part * TILE, 1.0, 0.0).astype(jnp.bfloat16)
                for part in range(WIDE // TILE)
            ],
            axis=1,
        )
        hot = jnp.concatenate([hot, hot, hot], axis=0)
        value = jnp.concatenate(split_exact(pulled[corner]), axis=1)
        masked = []
        for h in range(wides):
            mask = jnp.where(wide == h, 1.0, 0.0).astype(jnp.bfloat16)
            mask = jnp.concatenate([mask] * (rows // 16), axis=0)
            masked.append(value * jnp.concatenate([mask] * 3, axis=1))
        masked = jnp.concatenate(masked, axis=0)
        total[...] += jnp.dot(masked, hot, preferred_element_type=jnp.float32)

    def elements(step):
        for part in range(WIDE // TILE):
            lanes = slice(part * TILE, (part + 1) * TILE)
            place = pl.multiple_of(step * WIDE + part * TILE, TILE)
            for r in range(rows // 16):
                band = slice(r * 16, (r + 1) * 16)
                values = [held[c, band, lanes] for c in range(corner_count)]
                sums = [None] * corner_count
                for g in range(gauss_count):
                    coefficient = [
                        sensitivity[g, c : c + 1, pl.ds(place, TILE)] for c in range(corner_count)
                    ]
                    observed = values[0] * coefficient[0]
                    for c in range(1, corner_count):
                        observed = observed + values[c] * coefficient[c]
                    observed = observed * weight[g : g + 1, pl.ds(place, TILE)]
                    for c in range(corner_count):
                        term = observed * coefficient[c]
                        sums[c] = term if g == 0 else sums[c] + term
                for c in range(corner_count):
                    pulled[c, band, lanes] = sums[c]

    load_nodes(0, 0)

    def first(corner, carry):
        gather(corner, 0)
        return carry

    lax.fori_loop(0, corner_count, first, 0)

    def block(step, carry):
        turn = lax.rem(step, 2)
        elements(step)
        load_columns(step)
        load_nodes(jnp.minimum(step + 1, blocks - 1), 1 - turn)

        def both(corner, carry):
            scatter(corner, turn)
            gather(corner, 1 - turn)
            return carry

        lax.fori_loop(0, corner_count, both, 0)
        return carry

    lax.fori_loop(0, blocks, block, 0)
    for h in range(wides):
        out[:, h * WIDE : (h + 1) * WIDE] = total[h * rows : (h + 1) * rows, :]


def padded(array, dim, multiple):
    extra = -array.shape[dim] % multiple
    if not extra:
        return array
    return jnp.pad(array, [(0, extra if d == dim else 0) for d in range(array.ndim)])


def element_images(extended, sensitivity, obs_weight, local):
    corner_count = local.shape[0]
    local = padded(local, 1, WIDE)
    sensitivity = padded(sensitivity, 2, WIDE)
    obs_weight = padded(obs_weight, 1, WIDE)
    rows, nodes = extended.shape
    vmem = pl.BlockSpec(memory_space=pltpu.VMEM)
    return pl.pallas_call(
        element_kernel,
        out_shape=jax.ShapeDtypeStruct((rows, nodes), jnp.float32),
        in_specs=[vmem] * 5,
        out_specs=vmem,
        scratch_shapes=[
            pltpu.VMEM((2, corner_count, 16, WIDE), jnp.int32),
            pltpu.VMEM((corner_count, WIDE, TILE), jnp.int32),
            pltpu.VMEM((corner_count, rows, WIDE), jnp.float32),
            pltpu.VMEM((corner_count, rows, WIDE), jnp.float32),
            pltpu.VMEM((nodes // WIDE * rows, WIDE), jnp.float32),
        ],
        compiler_params=pltpu.CompilerParams(vmem_limit_bytes=48 * 1024 * 1024),
        name="elements",
    )(extended, local, local.T, sensitivity, obs_weight)


def halo_kernel(space_axis_size, halo, probes, extended, send_sem, recv_sem):
    s_me = lax.axis_index("space")
    rows, nodes = probes.shape
    has_lower, has_upper = s_me > 0, s_me < space_axis_size - 1
    barrier = pltpu.get_barrier_semaphore()

    def greet(to):
        pl.semaphore_signal(barrier, inc=1, device_id={"space": to}, device_id_type=MESH)

    pl.when(has_lower)(lambda: greet(s_me - 1))
    pl.when(has_upper)(lambda: greet(s_me + 1))
    pl.semaphore_wait(barrier, jnp.where(has_lower, 1, 0) + jnp.where(has_upper, 1, 0))

    def copy(side):
        low = side == 0
        return pltpu.make_async_remote_copy(
            src_ref=probes.at[:, :halo] if low else probes.at[:, nodes - halo :],
            dst_ref=extended.at[:rows, halo + nodes : halo + nodes + halo]
            if low
            else extended.at[:rows, :halo],
            send_sem=send_sem.at[side],
            recv_sem=recv_sem.at[side],
            device_id={"space": s_me - 1 if low else s_me + 1},
            device_id_type=MESH,
        )

    pl.when(has_lower)(lambda: copy(0).start())
    pl.when(has_upper)(lambda: copy(1).start())
    extended[:rows, halo : halo + nodes] = probes[...]
    if extended.shape[0] > rows:
        extended[rows:, :] = jnp.zeros_like(extended[rows:, :])
    end = halo + nodes + halo
    if extended.shape[1] > end:
        extended[:rows, end:] = jnp.zeros_like(extended[:rows, end:])

    @pl.when(jnp.logical_not(has_lower))
    def _():
        extended[:rows, :halo] = jnp.zeros((rows, halo), jnp.float32)

    @pl.when(jnp.logical_not(has_upper))
    def _():
        extended[:rows, halo + nodes : end] = jnp.zeros((rows, halo), jnp.float32)

    @pl.when(has_lower)
    def _():
        copy(1).wait_recv()
        copy(0).wait_send()

    @pl.when(has_upper)
    def _():
        copy(0).wait_recv()
        copy(1).wait_send()


def with_halo(probes, halo):
    space_axis_size = lax.axis_size("space")
    rows, nodes = probes.shape
    vmem = pl.BlockSpec(memory_space=pltpu.VMEM)
    return pl.pallas_call(
        functools.partial(halo_kernel, space_axis_size, halo),
        out_shape=jax.ShapeDtypeStruct(
            (rows + -rows % 16, nodes + 2 * halo + -(nodes + 2 * halo) % WIDE), jnp.float32
        ),
        in_specs=[vmem],
        out_specs=vmem,
        scratch_shapes=[pltpu.SemaphoreType.DMA((2,)), pltpu.SemaphoreType.DMA((2,))],
        compiler_params=pltpu.CompilerParams(
            collective_id=1, has_side_effects=True, vmem_limit_bytes=16 * 1024 * 1024
        ),
        name="halo",
    )(probes)


BAND = 8


def exact_dot(left, right, left_dim=1, right_dim=0):
    return lax.dot_general(
        left,
        right,
        (((left_dim,), (right_dim,)), ((), ())),
        precision=highest,
        preferred_element_type=jnp.float32,
    )


def small_factor(entry):
    entry = dict(entry)
    inverse = {}
    for m in range(BAND):
        root = lax.rsqrt(entry[m, m])
        for i in range(m + 1, BAND):
            entry[i, m] = entry[i, m] * root
        for i in range(m + 1, BAND):
            for k in range(m + 1, i + 1):
                entry[i, k] = entry[i, k] - entry[i, m] * entry[k, m]
        for k in range(m):
            term = entry[m, k] * inverse[k, k]
            for n in range(k + 1, m):
                term = term + entry[m, n] * inverse[n, k]
            inverse[m, k] = -term * root
        inverse[m, m] = root
    return inverse


def lane_columns(band, start):
    return [
        jnp.broadcast_to(band[:, start + m : start + m + 1], band.shape) for m in range(BAND)
    ]


def row_sum(value):
    return jnp.broadcast_to(jnp.sum(value, axis=0, keepdims=True), value.shape)


def block_entries(band, start):
    columns = lane_columns(band, start)
    return {
        (i, m): jnp.broadcast_to(columns[m][i : i + 1, :], band.shape)
        for m in range(BAND)
        for i in range(m, BAND)
    }


def factored(gram):
    size = gram.shape[0]
    row = lax.broadcasted_iota(jnp.int32, (size, size), 0)
    column = lax.broadcasted_iota(jnp.int32, (size, size), 1)
    unit = jnp.where(row == column, 1.0, 0.0)
    level = lax.broadcasted_iota(jnp.int32, (BAND, size), 0)
    count = size // BAND
    bands = []
    for j in range(count):
        part = slice(j * BAND, (j + 1) * BAND)
        bands.append((gram[part], unit[part]))
    entry = block_entries(bands[0][0], 0)
    for j in range(count):
        left, right = bands[j]
        inverse = small_factor(entry)
        new_left = new_right = None
        for m in range(BAND):
            weights = jnp.zeros_like(left)
            for i in range(m, BAND):
                weights = jnp.where(level == i, inverse[i, m], weights)
            add_left = weights * left[m : m + 1, :]
            add_right = weights * right[m : m + 1, :]
            new_left = add_left if m == 0 else new_left + add_left
            new_right = add_right if m == 0 else new_right + add_right
        bands[j] = (new_left, new_right)
        if j + 1 < count:
            columns = lane_columns(new_left, (j + 1) * BAND)
            left, right = bands[j + 1]
            entry = block_entries(left, (j + 1) * BAND)
            for i, m in entry:
                entry[i, m] = entry[i, m] - row_sum(columns[i] * columns[m])
            for i in range(BAND):
                left = jnp.where(level == i, left - row_sum(columns[i] * new_left), left)
                right = jnp.where(level == i, right - row_sum(columns[i] * new_right), right)
            bands[j + 1] = (left, right)
        if j + 2 < count:
            multipliers = new_left.T
            away_left = exact_dot(multipliers, new_left)
            away_right = exact_dot(multipliers, new_right)
            for i in range(j + 2, count):
                part = slice(i * BAND, (i + 1) * BAND)
                bands[i] = (bands[i][0] - away_left[part], bands[i][1] - away_right[part])
    upper = jnp.concatenate([band[0] for band in bands], axis=0)
    lower = jnp.concatenate([band[1] for band in bands], axis=0)
    return jnp.where(row <= column, upper, 0.0), lower


def send_all(axis, count, me, source, target, send_sem, recv_sem):
    copies = []
    for d in range(1, count):
        to = lax.rem(me + d, count)
        copy = pltpu.make_async_remote_copy(
            src_ref=source(to),
            dst_ref=target,
            send_sem=send_sem.at[d],
            recv_sem=recv_sem.at[d],
            device_id={axis: to},
            device_id_type=MESH,
        )
        copy.start()
        copies.append(copy)
    return copies


def wait_all(copies):
    for copy in copies:
        copy.wait()


def orthonormal_kernel(
    probe_axis_size, space_axis_size, halo, summed, probes, prior, basis, factor,
    images, rim, mine, block, everything, rows_of, partial, strips, bands, grams,
    rim_send, rim_recv, move_send, move_recv, rest_send, rest_recv, a_send, a_recv, b_send, b_recv, c_send, c_recv,
):
    p_me, s_me = lax.axis_index("probe"), lax.axis_index("space")
    rows, nodes = probes.shape
    size = rows * probe_axis_size
    share = nodes // probe_axis_size
    strip = size // space_axis_size
    scale = math.sqrt(float(nodes * space_axis_size))

    barrier = pltpu.get_barrier_semaphore()
    for d in range(1, space_axis_size):
        to = lax.rem(s_me + d, space_axis_size)
        pl.semaphore_signal(barrier, inc=1, device_id={"space": to}, device_id_type=MESH)
    for d in range(1, probe_axis_size):
        to = lax.rem(p_me + d, probe_axis_size)
        pl.semaphore_signal(barrier, inc=1, device_id={"probe": to}, device_id_type=MESH)
    pl.semaphore_wait(barrier, space_axis_size + probe_axis_size - 2)

    end = halo + nodes + halo

    def rim_copy(side):
        source = summed.at[:rows, :halo] if side == 0 else summed.at[:rows, halo + nodes : end]
        return pltpu.make_async_remote_copy(
            src_ref=source,
            dst_ref=rim.at[side],
            send_sem=rim_send.at[side],
            recv_sem=rim_recv.at[side],
            device_id={"space": s_me - 1 if side == 0 else s_me + 1},
            device_id_type=MESH,
        )

    has_lower, has_upper = s_me > 0, s_me < space_axis_size - 1
    pl.when(has_lower)(lambda: rim_copy(0).start())
    pl.when(has_upper)(lambda: rim_copy(1).start())
    images[...] = summed[:rows, halo : halo + nodes] + prior[...] * probes[...]

    @pl.when(has_upper)
    def _():
        rim_copy(0).wait_recv()
        images[:, nodes - halo :] += rim[0]

    @pl.when(has_lower)
    def _():
        rim_copy(1).wait_recv()
        images[:, :halo] += rim[1]

    def lanes(index):
        return pl.ds(pl.multiple_of(index * share, share), share)

    copies = send_all(
        "probe", probe_axis_size, p_me, lambda to: images.at[:, lanes(to)],
        mine.at[p_me], move_send, move_recv,
    )
    mine[p_me] = images[:, lanes(p_me)]
    wait_all(copies)

    def summed_gram(turn, value):
        for s in range(space_axis_size):
            partial[turn, s] = value[s * strip : (s + 1) * strip]
        copies = send_all(
            "space", space_axis_size, s_me, lambda to: partial.at[turn, to],
            strips.at[turn, s_me], a_send.at[turn], a_recv.at[turn],
        )
        strips[turn, s_me] = partial[turn, s_me]
        wait_all(copies)
        total = strips[turn, 0]
        for s in range(1, space_axis_size):
            total = total + strips[turn, s]
        bands[turn, p_me] = total
        copies = send_all(
            "probe", probe_axis_size, p_me, lambda to: bands.at[turn, p_me],
            bands.at[turn, p_me], b_send.at[turn], b_recv.at[turn],
        )
        wait_all(copies)
        total = bands[turn, 0]
        for p in range(1, probe_axis_size):
            total = total + bands[turn, p]
        grams[turn, s_me] = total
        copies = send_all(
            "space", space_axis_size, s_me, lambda to: grams.at[turn, s_me],
            grams.at[turn, s_me], c_send.at[turn], c_recv.at[turn],
        )
        wait_all(copies)
        return jnp.concatenate([grams[turn, s] for s in range(space_axis_size)], axis=0)

    whole = mine[...].reshape(size, share)
    gram_first = summed_gram(0, exact_dot(whole, whole, 1, 1))
    rest = []
    for e in range(1, probe_axis_size):
        for d in range(1, probe_axis_size):
            to = lax.rem(p_me + d, probe_axis_size)
            place = lanes(lax.rem(to + e, probe_axis_size))
            copy = pltpu.make_async_remote_copy(
                src_ref=images.at[:, place],
                dst_ref=everything.at[p_me, :, place],
                send_sem=rest_send.at[d, e],
                recv_sem=rest_recv.at[d, e],
                device_id={"probe": to},
                device_id_type=MESH,
            )
            copy.start()
            rest.append(copy)
    everything[:, :, lanes(p_me)] = mine[...]
    for e in range(1, probe_axis_size):
        place = lanes(lax.rem(p_me + e, probe_axis_size))
        everything[p_me, :, place] = images[:, place]
    upper_first, inverse_first = factored(gram_first)
    block[...] = exact_dot(inverse_first, mine[...].reshape(size, share))
    first = block[...]
    upper_second, inverse_second = factored(summed_gram(1, exact_dot(first, first, 1, 1)))
    factor[...] = exact_dot(upper_second, upper_first) / scale
    rows_of[...] = exact_dot(inverse_second * scale, inverse_first)
    own = rows_of[pl.ds(pl.multiple_of(p_me * rows, rows), rows), :]
    wait_all(rest)
    basis[...] = exact_dot(own, everything[...].reshape(size, nodes))
    pl.when(has_lower)(lambda: rim_copy(0).wait_send())
    pl.when(has_upper)(lambda: rim_copy(1).wait_send())


def orthonormal(summed, probes, prior, halo):
    probe_axis_size, space_axis_size = lax.axis_size("probe"), lax.axis_size("space")
    rows, nodes = probes.shape
    size, share = rows * probe_axis_size, nodes // probe_axis_size
    strip = size // space_axis_size
    vmem = pl.BlockSpec(memory_space=pltpu.VMEM)
    dma = pltpu.SemaphoreType.DMA
    return pl.pallas_call(
        functools.partial(orthonormal_kernel, probe_axis_size, space_axis_size, halo),
        out_shape=(
            jax.ShapeDtypeStruct((rows, nodes), jnp.float32),
            jax.ShapeDtypeStruct((size, size), jnp.float32),
        ),
        in_specs=[vmem] * 3,
        out_specs=(vmem, vmem),
        scratch_shapes=[
            pltpu.VMEM((rows, nodes), jnp.float32),
            pltpu.VMEM((2, rows, halo), jnp.float32),
            pltpu.VMEM((probe_axis_size, rows, share), jnp.float32),
            pltpu.VMEM((size, share), jnp.float32),
            pltpu.VMEM((probe_axis_size, rows, nodes), jnp.float32),
            pltpu.VMEM((size, size), jnp.float32),
            pltpu.VMEM((2, space_axis_size, strip, size), jnp.float32),
            pltpu.VMEM((2, space_axis_size, strip, size), jnp.float32),
            pltpu.VMEM((2, probe_axis_size, strip, size), jnp.float32),
            pltpu.VMEM((2, space_axis_size, strip, size), jnp.float32),
            dma((2,)),
            dma((2,)),
            dma((probe_axis_size,)),
            dma((probe_axis_size,)),
            dma((probe_axis_size, probe_axis_size)),
            dma((probe_axis_size, probe_axis_size)),
            dma((2, space_axis_size)),
            dma((2, space_axis_size)),
            dma((2, probe_axis_size)),
            dma((2, probe_axis_size)),
            dma((2, space_axis_size)),
            dma((2, space_axis_size)),
        ],
        compiler_params=pltpu.CompilerParams(
            collective_id=0, has_side_effects=True, vmem_limit_bytes=48 * 1024 * 1024
        ),
        name="orthonormal",
    )(summed, probes, prior)


def on_device(probes, sensitivity, obs_weight, prior_weight, connectivity):
    extended = with_halo(probes, HALO)
    summed = element_images(extended, sensitivity, obs_weight, connectivity)
    return orthonormal(summed, probes, prior_weight[None, :], HALO)


def solution(mesh):
    return jax.shard_map(
        on_device,
        mesh=mesh,
        in_specs=(
            P("probe", "space"),
            P(None, None, "space"),
            P(None, "space"),
            P("space"),
            P(None, "space"),
        ),
        out_specs=(P("probe", "space"), P()),
        check_vma=False,
    )
```

```python
import functools
import math

import jax
import jax.numpy as jnp
from jax import lax
from jax.experimental import pallas as pl
from jax.experimental.pallas import tpu as pltpu
from jax.sharding import PartitionSpec as P

HALO = 128


highest = lax.Precision.HIGHEST


TILE = 128
WIDE = 256


def split_exact(value):
    high = value.astype(jnp.bfloat16)
    rest = value - high.astype(jnp.float32)
    middle = rest.astype(jnp.bfloat16)
    low = (rest - middle.astype(jnp.float32)).astype(jnp.bfloat16)
    return high, middle, low


MESH = pl.DeviceIdType.MESH


def element_kernel(
    extended, local, corner_column, sensitivity, weight, out, node, spread, held, pulled, total
):
    gauss_count, corner_count, element_count = sensitivity.shape
    rows, nodes = extended.shape
    tiles, wides = nodes // TILE, nodes // WIDE
    blocks = element_count // WIDE
    together = math.gcd(corner_count, 4)
    total[...] = jnp.zeros_like(total)

    def load_nodes(step, turn):
        start = pl.multiple_of(step * WIDE, WIDE)
        for c in range(corner_count):
            index = local[c : c + 1, pl.ds(start, WIDE)]
            node[turn, c] = jnp.broadcast_to(index, (16, WIDE))

    def load_columns(step):
        start = pl.multiple_of(step * WIDE, WIDE)
        for c in range(corner_count):
            column = corner_column[pl.ds(start, WIDE), c : c + 1]
            spread[c] = jnp.broadcast_to(column & (WIDE - 1), (WIDE, TILE))

    def gather(corner, turn):
        for part in range(WIDE // TILE):
            lanes = slice(part * TILE, (part + 1) * TILE)
            index = node[turn, corner, 0:8, lanes]
            lane, tile = index & (TILE - 1), index >> 7
            found = [jnp.zeros((8, TILE), jnp.float32)] * (rows // 8)
            for t in range(tiles):
                here = tile == t
                for r in range(rows // 8):
                    source = extended[r * 8 : (r + 1) * 8, t * TILE : (t + 1) * TILE]
                    picked = jnp.take_along_axis(source, lane, axis=1, mode="promise_in_bounds")
                    found[r] = jnp.where(here, picked, found[r])
            for r in range(rows // 8):
                held[corner, r * 8 : (r + 1) * 8, lanes] = found[r]

    def scatter_terms(corner, turn):
        wide = node[turn, corner] >> 8
        lane = spread[corner]
        count = lax.broadcasted_iota(jnp.int32, (WIDE, TILE), 1)
        hot = jnp.concatenate(
            [
                jnp.where(lane == count + part * TILE, 1.0, 0.0).astype(jnp.bfloat16)
                for part in range(WIDE // TILE)
            ],
            axis=1,
        )
        hot = jnp.concatenate([hot, hot, hot], axis=0)
        value = jnp.concatenate(split_exact(pulled[corner]), axis=1)
        masked = []
        for h in range(wides):
            mask = jnp.where(wide == h, 1.0, 0.0).astype(jnp.bfloat16)
            mask = jnp.concatenate([mask] * (rows // 16), axis=0)
            masked.append(value * jnp.concatenate([mask] * 3, axis=1))
        return jnp.concatenate(masked, axis=0), hot

    def scatter(corners, turn):
        terms = [scatter_terms(corner, turn) for corner in corners]
        masked = jnp.concatenate([term[0] for term in terms], axis=1)
        hot = jnp.concatenate([term[1] for term in terms], axis=0)
        total[...] += jnp.dot(masked, hot, preferred_element_type=jnp.float32)

    def elements(step):
        for part in range(WIDE // TILE):
            lanes = slice(part * TILE, (part + 1) * TILE)
            place = pl.multiple_of(step * WIDE + part * TILE, TILE)
            for r in range(rows // 16):
                band = slice(r * 16, (r + 1) * 16)
                values = [held[c, band, lanes] for c in range(corner_count)]
                sums = [None] * corner_count
                for g in range(gauss_count):
                    coefficient = [
                        sensitivity[g, c : c + 1, pl.ds(place, TILE)] for c in range(corner_count)
                    ]
                    observed = values[0] * coefficient[0]
                    for c in range(1, corner_count):
                        observed = observed + values[c] * coefficient[c]
                    observed = observed * weight[g : g + 1, pl.ds(place, TILE)]
                    for c in range(corner_count):
                        term = observed * coefficient[c]
                        sums[c] = term if g == 0 else sums[c] + term
                for c in range(corner_count):
                    pulled[c, band, lanes] = sums[c]

    load_nodes(0, 0)

    def first(corner, carry):
        gather(corner, 0)
        return carry

    lax.fori_loop(0, corner_count, first, 0)

    def block(step, carry):
        turn = lax.rem(step, 2)
        elements(step)
        load_columns(step)
        load_nodes(jnp.minimum(step + 1, blocks - 1), 1 - turn)

        def both(step, carry):
            corners = [step * together + c for c in range(together)]
            scatter(corners, turn)
            for corner in corners:
                gather(corner, 1 - turn)
            return carry

        lax.fori_loop(0, corner_count // together, both, 0)
        return carry

    lax.fori_loop(0, blocks, block, 0)
    for h in range(wides):
        out[:, h * WIDE : (h + 1) * WIDE] = total[h * rows : (h + 1) * rows, :]


def padded(array, dim, multiple):
    extra = -array.shape[dim] % multiple
    if not extra:
        return array
    return jnp.pad(array, [(0, extra if d == dim else 0) for d in range(array.ndim)])


def element_images(extended, sensitivity, obs_weight, local):
    corner_count = local.shape[0]
    local = padded(local, 1, WIDE)
    sensitivity = padded(sensitivity, 2, WIDE)
    obs_weight = padded(obs_weight, 1, WIDE)
    rows, nodes = extended.shape
    vmem = pl.BlockSpec(memory_space=pltpu.VMEM)
    return pl.pallas_call(
        element_kernel,
        out_shape=jax.ShapeDtypeStruct((rows, nodes), jnp.float32),
        in_specs=[vmem] * 5,
        out_specs=vmem,
        scratch_shapes=[
            pltpu.VMEM((2, corner_count, 16, WIDE), jnp.int32),
            pltpu.VMEM((corner_count, WIDE, TILE), jnp.int32),
            pltpu.VMEM((corner_count, rows, WIDE), jnp.float32),
            pltpu.VMEM((corner_count, rows, WIDE), jnp.float32),
            pltpu.VMEM((nodes // WIDE * rows, WIDE), jnp.float32),
        ],
        compiler_params=pltpu.CompilerParams(vmem_limit_bytes=48 * 1024 * 1024),
        name="elements",
    )(extended, local, local.T, sensitivity, obs_weight)


def halo_kernel(space_axis_size, halo, probes, extended, send_sem, recv_sem):
    s_me = lax.axis_index("space")
    rows, nodes = probes.shape
    has_lower, has_upper = s_me > 0, s_me < space_axis_size - 1
    barrier = pltpu.get_barrier_semaphore()

    def greet(to):
        pl.semaphore_signal(barrier, inc=1, device_id={"space": to}, device_id_type=MESH)

    pl.when(has_lower)(lambda: greet(s_me - 1))
    pl.when(has_upper)(lambda: greet(s_me + 1))
    pl.semaphore_wait(barrier, jnp.where(has_lower, 1, 0) + jnp.where(has_upper, 1, 0))

    def copy(side):
        low = side == 0
        return pltpu.make_async_remote_copy(
            src_ref=probes.at[:, :halo] if low else probes.at[:, nodes - halo :],
            dst_ref=extended.at[:rows, halo + nodes : halo + nodes + halo]
            if low
            else extended.at[:rows, :halo],
            send_sem=send_sem.at[side],
            recv_sem=recv_sem.at[side],
            device_id={"space": s_me - 1 if low else s_me + 1},
            device_id_type=MESH,
        )

    pl.when(has_lower)(lambda: copy(0).start())
    pl.when(has_upper)(lambda: copy(1).start())
    extended[:rows, halo : halo + nodes] = probes[...]
    if extended.shape[0] > rows:
        extended[rows:, :] = jnp.zeros_like(extended[rows:, :])
    end = halo + nodes + halo
    if extended.shape[1] > end:
        extended[:rows, end:] = jnp.zeros_like(extended[:rows, end:])

    @pl.when(jnp.logical_not(has_lower))
    def _():
        extended[:rows, :halo] = jnp.zeros((rows, halo), jnp.float32)

    @pl.when(jnp.logical_not(has_upper))
    def _():
        extended[:rows, halo + nodes : end] = jnp.zeros((rows, halo), jnp.float32)

    @pl.when(has_lower)
    def _():
        copy(1).wait_recv()
        copy(0).wait_send()

    @pl.when(has_upper)
    def _():
        copy(0).wait_recv()
        copy(1).wait_send()


def with_halo(probes, halo):
    space_axis_size = lax.axis_size("space")
    rows, nodes = probes.shape
    vmem = pl.BlockSpec(memory_space=pltpu.VMEM)
    return pl.pallas_call(
        functools.partial(halo_kernel, space_axis_size, halo),
        out_shape=jax.ShapeDtypeStruct(
            (rows + -rows % 16, nodes + 2 * halo + -(nodes + 2 * halo) % WIDE), jnp.float32
        ),
        in_specs=[vmem],
        out_specs=vmem,
        scratch_shapes=[pltpu.SemaphoreType.DMA((2,)), pltpu.SemaphoreType.DMA((2,))],
        compiler_params=pltpu.CompilerParams(
            collective_id=1, has_side_effects=True, vmem_limit_bytes=16 * 1024 * 1024
        ),
        name="halo",
    )(probes)


BAND = 8


def exact_dot(left, right, left_dim=1, right_dim=0):
    return lax.dot_general(
        left,
        right,
        (((left_dim,), (right_dim,)), ((), ())),
        precision=highest,
        preferred_element_type=jnp.float32,
    )


def small_factor(entry):
    entry = dict(entry)
    inverse = {}
    for m in range(BAND):
        root = lax.rsqrt(entry[m, m])
        for i in range(m + 1, BAND):
            entry[i, m] = entry[i, m] * root
        for i in range(m + 1, BAND):
            for k in range(m + 1, i + 1):
                entry[i, k] = entry[i, k] - entry[i, m] * entry[k, m]
        for k in range(m):
            term = entry[m, k] * inverse[k, k]
            for n in range(k + 1, m):
                term = term + entry[m, n] * inverse[n, k]
            inverse[m, k] = -term * root
        inverse[m, m] = root
    return inverse


def lane_columns(band, start):
    return [
        jnp.broadcast_to(band[:, start + m : start + m + 1], band.shape) for m in range(BAND)
    ]


def row_sum(value):
    return jnp.broadcast_to(jnp.sum(value, axis=0, keepdims=True), value.shape)


def block_entries(band, start):
    columns = lane_columns(band, start)
    return {
        (i, m): jnp.broadcast_to(columns[m][i : i + 1, :], band.shape)
        for m in range(BAND)
        for i in range(m, BAND)
    }


def factored(gram):
    size = gram.shape[0]
    row = lax.broadcasted_iota(jnp.int32, (size, size), 0)
    column = lax.broadcasted_iota(jnp.int32, (size, size), 1)
    unit = jnp.where(row == column, 1.0, 0.0)
    level = lax.broadcasted_iota(jnp.int32, (BAND, size), 0)
    count = size // BAND
    bands = []
    for j in range(count):
        part = slice(j * BAND, (j + 1) * BAND)
        bands.append((gram[part], unit[part]))
    entry = block_entries(bands[0][0], 0)
    for j in range(count):
        left, right = bands[j]
        inverse = small_factor(entry)
        new_left = new_right = None
        for m in range(BAND):
            weights = jnp.zeros_like(left)
            for i in range(m, BAND):
                weights = jnp.where(level == i, inverse[i, m], weights)
            add_left = weights * left[m : m + 1, :]
            add_right = weights * right[m : m + 1, :]
            new_left = add_left if m == 0 else new_left + add_left
            new_right = add_right if m == 0 else new_right + add_right
        bands[j] = (new_left, new_right)
        if j + 1 < count:
            columns = lane_columns(new_left, (j + 1) * BAND)
            left, right = bands[j + 1]
            entry = block_entries(left, (j + 1) * BAND)
            for i, m in entry:
                entry[i, m] = entry[i, m] - row_sum(columns[i] * columns[m])
            for i in range(BAND):
                left = jnp.where(level == i, left - row_sum(columns[i] * new_left), left)
                right = jnp.where(level == i, right - row_sum(columns[i] * new_right), right)
            bands[j + 1] = (left, right)
        if j + 2 < count:
            multipliers = new_left.T
            away_left = exact_dot(multipliers, new_left)
            away_right = exact_dot(multipliers, new_right)
            for i in range(j + 2, count):
                part = slice(i * BAND, (i + 1) * BAND)
                bands[i] = (bands[i][0] - away_left[part], bands[i][1] - away_right[part])
    upper = jnp.concatenate([band[0] for band in bands], axis=0)
    lower = jnp.concatenate([band[1] for band in bands], axis=0)
    return jnp.where(row <= column, upper, 0.0), lower


def send_all(axis, count, me, source, target, send_sem, recv_sem):
    copies = []
    for d in range(1, count):
        to = lax.rem(me + d, count)
        copy = pltpu.make_async_remote_copy(
            src_ref=source(to),
            dst_ref=target,
            send_sem=send_sem.at[d],
            recv_sem=recv_sem.at[d],
            device_id={axis: to},
            device_id_type=MESH,
        )
        copy.start()
        copies.append(copy)
    return copies


def wait_all(copies):
    for copy in copies:
        copy.wait()


def orthonormal_kernel(
    probe_axis_size, space_axis_size, halo, summed, probes, prior, basis, factor,
    images, rim, mine, block, everything, rows_of, partial, strips, bands, grams,
    rim_send, rim_recv, move_send, move_recv, rest_send, rest_recv, a_send, a_recv, b_send, b_recv, c_send, c_recv,
):
    p_me, s_me = lax.axis_index("probe"), lax.axis_index("space")
    rows, nodes = probes.shape
    size = rows * probe_axis_size
    share = nodes // probe_axis_size
    strip = size // space_axis_size
    scale = math.sqrt(float(nodes * space_axis_size))

    barrier = pltpu.get_barrier_semaphore()
    for d in range(1, space_axis_size):
        to = lax.rem(s_me + d, space_axis_size)
        pl.semaphore_signal(barrier, inc=1, device_id={"space": to}, device_id_type=MESH)
    for d in range(1, probe_axis_size):
        to = lax.rem(p_me + d, probe_axis_size)
        pl.semaphore_signal(barrier, inc=1, device_id={"probe": to}, device_id_type=MESH)
    pl.semaphore_wait(barrier, space_axis_size + probe_axis_size - 2)

    end = halo + nodes + halo

    def rim_copy(side):
        source = summed.at[:rows, :halo] if side == 0 else summed.at[:rows, halo + nodes : end]
        return pltpu.make_async_remote_copy(
            src_ref=source,
            dst_ref=rim.at[side],
            send_sem=rim_send.at[side],
            recv_sem=rim_recv.at[side],
            device_id={"space": s_me - 1 if side == 0 else s_me + 1},
            device_id_type=MESH,
        )

    has_lower, has_upper = s_me > 0, s_me < space_axis_size - 1
    pl.when(has_lower)(lambda: rim_copy(0).start())
    pl.when(has_upper)(lambda: rim_copy(1).start())
    images[...] = summed[:rows, halo : halo + nodes] + prior[...] * probes[...]

    def lanes(index):
        return pl.ds(pl.multiple_of(index * share, share), share)

    def quarter_copy(d):
        to = lax.rem(p_me + d, probe_axis_size)
        return pltpu.make_async_remote_copy(
            src_ref=images.at[:, lanes(to)],
            dst_ref=mine.at[p_me],
            send_sem=move_send.at[d],
            recv_sem=move_recv.at[d],
            device_id={"probe": to},
            device_id_type=MESH,
        )

    def at_rim(d):
        to = lax.rem(p_me + d, probe_axis_size)
        return jnp.logical_or(to == 0, to == probe_axis_size - 1)

    for d in range(1, probe_axis_size):
        pl.when(jnp.logical_not(at_rim(d)))(lambda d=d: quarter_copy(d).start())

    @pl.when(has_upper)
    def _():
        rim_copy(0).wait_recv()
        images[:, nodes - halo :] += rim[0]

    @pl.when(has_lower)
    def _():
        rim_copy(1).wait_recv()
        images[:, :halo] += rim[1]

    for d in range(1, probe_axis_size):
        pl.when(at_rim(d))(lambda d=d: quarter_copy(d).start())
    mine[p_me] = images[:, lanes(p_me)]
    for d in range(1, probe_axis_size):
        quarter_copy(d).wait()

    def summed_gram(turn, value):
        for s in range(space_axis_size):
            partial[turn, s] = value[s * strip : (s + 1) * strip]
        copies = send_all(
            "space", space_axis_size, s_me, lambda to: partial.at[turn, to],
            strips.at[turn, s_me], a_send.at[turn], a_recv.at[turn],
        )
        strips[turn, s_me] = partial[turn, s_me]
        wait_all(copies)
        total = strips[turn, 0]
        for s in range(1, space_axis_size):
            total = total + strips[turn, s]
        bands[turn, p_me] = total
        copies = send_all(
            "probe", probe_axis_size, p_me, lambda to: bands.at[turn, p_me],
            bands.at[turn, p_me], b_send.at[turn], b_recv.at[turn],
        )
        wait_all(copies)
        total = bands[turn, 0]
        for p in range(1, probe_axis_size):
            total = total + bands[turn, p]
        grams[turn, s_me] = total
        copies = send_all(
            "space", space_axis_size, s_me, lambda to: grams.at[turn, s_me],
            grams.at[turn, s_me], c_send.at[turn], c_recv.at[turn],
        )
        wait_all(copies)
        return jnp.concatenate([grams[turn, s] for s in range(space_axis_size)], axis=0)

    whole = mine[...].reshape(size, share)
    gram_first = summed_gram(0, exact_dot(whole, whole, 1, 1))
    rest = []
    for e in range(1, probe_axis_size):
        for d in range(1, probe_axis_size):
            to = lax.rem(p_me + d, probe_axis_size)
            place = lanes(lax.rem(to + e, probe_axis_size))
            copy = pltpu.make_async_remote_copy(
                src_ref=images.at[:, place],
                dst_ref=everything.at[p_me, :, place],
                send_sem=rest_send.at[d, e],
                recv_sem=rest_recv.at[d, e],
                device_id={"probe": to},
                device_id_type=MESH,
            )
            copy.start()
            rest.append(copy)
    everything[:, :, lanes(p_me)] = mine[...]
    for e in range(1, probe_axis_size):
        place = lanes(lax.rem(p_me + e, probe_axis_size))
        everything[p_me, :, place] = images[:, place]
    upper_first, inverse_first = factored(gram_first)
    block[...] = exact_dot(inverse_first, mine[...].reshape(size, share))
    first = block[...]
    upper_second, inverse_second = factored(summed_gram(1, exact_dot(first, first, 1, 1)))
    factor[...] = exact_dot(upper_second, upper_first) / scale
    rows_of[...] = exact_dot(inverse_second * scale, inverse_first)
    own = rows_of[pl.ds(pl.multiple_of(p_me * rows, rows), rows), :]
    wait_all(rest)
    basis[...] = exact_dot(own, everything[...].reshape(size, nodes))
    pl.when(has_lower)(lambda: rim_copy(0).wait_send())
    pl.when(has_upper)(lambda: rim_copy(1).wait_send())


def orthonormal(summed, probes, prior, halo):
    probe_axis_size, space_axis_size = lax.axis_size("probe"), lax.axis_size("space")
    rows, nodes = probes.shape
    size, share = rows * probe_axis_size, nodes // probe_axis_size
    strip = size // space_axis_size
    vmem = pl.BlockSpec(memory_space=pltpu.VMEM)
    dma = pltpu.SemaphoreType.DMA
    return pl.pallas_call(
        functools.partial(orthonormal_kernel, probe_axis_size, space_axis_size, halo),
        out_shape=(
            jax.ShapeDtypeStruct((rows, nodes), jnp.float32),
            jax.ShapeDtypeStruct((size, size), jnp.float32),
        ),
        in_specs=[vmem] * 3,
        out_specs=(vmem, vmem),
        scratch_shapes=[
            pltpu.VMEM((rows, nodes), jnp.float32),
            pltpu.VMEM((2, rows, halo), jnp.float32),
            pltpu.VMEM((probe_axis_size, rows, share), jnp.float32),
            pltpu.VMEM((size, share), jnp.float32),
            pltpu.VMEM((probe_axis_size, rows, nodes), jnp.float32),
            pltpu.VMEM((size, size), jnp.float32),
            pltpu.VMEM((2, space_axis_size, strip, size), jnp.float32),
            pltpu.VMEM((2, space_axis_size, strip, size), jnp.float32),
            pltpu.VMEM((2, probe_axis_size, strip, size), jnp.float32),
            pltpu.VMEM((2, space_axis_size, strip, size), jnp.float32),
            dma((2,)),
            dma((2,)),
            dma((probe_axis_size,)),
            dma((probe_axis_size,)),
            dma((probe_axis_size, probe_axis_size)),
            dma((probe_axis_size, probe_axis_size)),
            dma((2, space_axis_size)),
            dma((2, space_axis_size)),
            dma((2, probe_axis_size)),
            dma((2, probe_axis_size)),
            dma((2, space_axis_size)),
            dma((2, space_axis_size)),
        ],
        compiler_params=pltpu.CompilerParams(
            collective_id=0, has_side_effects=True, vmem_limit_bytes=48 * 1024 * 1024
        ),
        name="orthonormal",
    )(summed, probes, prior)


def on_device(probes, sensitivity, obs_weight, prior_weight, connectivity):
    extended = with_halo(probes, HALO)
    summed = element_images(extended, sensitivity, obs_weight, connectivity)
    return orthonormal(summed, probes, prior_weight[None, :], HALO)


def solution(mesh):
    return jax.shard_map(
        on_device,
        mesh=mesh,
        in_specs=(
            P("probe", "space"),
            P(None, None, "space"),
            P(None, "space"),
            P("space"),
            P(None, "space"),
        ),
        out_specs=(P("probe", "space"), P()),
        check_vma=False,
    )
```
